512 devices in a mesh: depth: 64 (over y, x, core), tile: 8 (over z).
Axes of the slice: x: 4, y: 8, z: 8, core: 2. Of those that a mesh axis runs over, the one named last changes fastest.
Arguments:
- volume: bfloat16 [1024, 512, 1024], P('depth', 'tile'), may hold values from 0 to 1
- empty_slices: int32 [64, 8], P('depth'), may hold values from 0 to 16
- shear: int32 [2], replicated, may hold values from 1 to 7
- extinction: float32 [1], replicated, may hold values from 0.25 to 1
- palette: float32 [2, 3], replicated, may hold values from 0.2 to 1.5
Outputs:
- image: float32 [4, 512, 1024], P(None, 'tile')
The draws below stay inside these ranges and needn't reach their ends.
All inputs are finite; a program needn't handle non-finite values.
Results may differ from the reference program's by a relative error of at most 0.0003.
Values may be sent and summed in bfloat16 or wider, within the bound.
No kernel may reach another device: no remote copies, remote signals or barrier semaphores. Data moves between devices by JAX's collectives and lax.ppermute only.
A program may use at most 64 MiB of HBM per device.

```python
import math
import jax
import jax.numpy as jnp
from jax import lax

SLAB = 16
ROWS = 64
WIDTH = 1024
NZ = 1024
HEIGHT = 512
BRICKS_Z = 64
BRICKS_Y = 8


def with_ends(entries, rng, least, high):
    shape = entries.shape
    place = [jax.random.randint(jax.random.fold_in(rng, axis), (), 0, shape[axis]) for axis in range(len(shape))]
    entries = entries.at[tuple(place)].set(least)
    longest = shape.index(max(shape))
    place[longest] = (place[longest] + 1) % shape[longest]
    return entries.at[tuple(place)].set(high)


def block_scale(stream_key, extent, shards, least, high):
    loudness = 1.0
    for dim, parts in shards:
        draws = jax.random.uniform(jax.random.fold_in(jax.random.fold_in(stream_key, 6), dim), (parts,), jnp.float32, least / len(shards), high / len(shards))
        loudness = loudness * jnp.repeat(jnp.exp(draws), extent[dim] // parts).reshape((-1,) + (1,) * (len(extent) - 1 - dim))
    return loudness


def setup_inputs(seed: int = 0) -> dict:
    splits = jax.random.split(jax.random.key(seed), 6)
    return {
        "volume": jnp.clip(1.0 * jax.random.uniform(splits[0], (NZ, HEIGHT, WIDTH), jnp.float32) ** block_scale(splits[0], (NZ, HEIGHT, WIDTH), ((0, 64), (1, 8)), -0.2, 0.2), 0.0, 1.0).astype(jnp.bfloat16),
        "empty_slices": with_ends(jax.random.randint(splits[1], (BRICKS_Z, BRICKS_Y), 0, SLAB + 1), jax.random.fold_in(splits[1], 1), 0, SLAB).astype(jnp.int32),
        "shear": jax.random.randint(splits[2], (2,), 1, 8).astype(jnp.int32),
        "extinction": jnp.clip(jnp.exp(jax.random.uniform(splits[3], (1,), jnp.float32, math.log(0.25), math.log(1.0))), 0.25, 1.0),
        "palette": jnp.clip(jax.random.uniform(splits[4], (2, 3), jnp.float32, 0.2, 1.5), 0.2, 1.5),
    }


def resample(padded, shear, depth_pos, depth_total, row_span, width, out_rows):
    col_num = shear[0] * depth_pos * width
    col_den = 32 * depth_total
    col_shift = (col_num // col_den).astype(jnp.int32)
    col_frac = (col_num % col_den).astype(jnp.float32) / float(col_den)
    row_num = shear[1] * depth_pos * row_span
    row_den = 8 * depth_total
    row_shift = (row_num // row_den).astype(jnp.int32)
    row_frac = (row_num % row_den).astype(jnp.float32) / float(row_den)
    col_pad = width // 4

    def pick_at(row_step, col_step):
        start_row = (row_span - row_shift - row_step).astype(jnp.int32)
        start_col = (col_pad - col_shift - col_step).astype(jnp.int32)
        return lax.dynamic_slice(padded, (start_row, start_col), (out_rows, width))

    upper_line = (1.0 - col_frac) * pick_at(0, 0) + col_frac * pick_at(0, 1)
    lower_line = (1.0 - col_frac) * pick_at(1, 0) + col_frac * pick_at(1, 1)
    return (1.0 - row_frac) * upper_line + row_frac * lower_line


def classify(sample, extinction, palette, depth_total):
    sigma = extinction[0] * 4.0 / depth_total
    alpha = 1.0 - jnp.exp(-sigma * sample)
    emitted = alpha[None] * (palette[0][:, None, None] + palette[1][:, None, None] * sample[None])
    return alpha, emitted


def reference(volume, empty_slices, shear, extinction, palette):
    col_pad = WIDTH // 4

    def advance(carry, inputs):
        color, trans = carry
        plane, depth_pos = inputs
        counts = lax.dynamic_index_in_dim(empty_slices, depth_pos // SLAB, 0, keepdims=False)
        row_counts = jnp.repeat(counts, ROWS)
        live = (depth_pos % SLAB) >= row_counts
        values = jnp.where(live[:, None], plane.astype(jnp.float32), jnp.float32(0.0))
        padded = jnp.pad(values, ((ROWS, 0), (col_pad, 0)))
        sample = resample(padded, shear, depth_pos, NZ, ROWS, WIDTH, HEIGHT)
        alpha, emitted = classify(sample, extinction, palette, NZ)
        color = color + trans[None] * emitted
        trans = trans * (1.0 - alpha)
        return (color, trans), None

    start = (jnp.zeros((3, HEIGHT, WIDTH), jnp.float32), jnp.ones((HEIGHT, WIDTH), jnp.float32))
    (color, trans), _ = lax.scan(advance, start, (volume, jnp.arange(NZ, dtype=jnp.int32)))
    return jnp.concatenate([color, (1.0 - trans)[None]], axis=0)
```

```python
import functools
import math

import jax
import jax.numpy as jnp
from jax import lax
from jax.experimental import pallas as pl
from jax.experimental.pallas import tpu as pltpu
from jax.sharding import PartitionSpec as P

SLAB = 16
ROWS = 64
WIDTH = 1024
LANES = 128
BLOCKS = WIDTH // LANES
DEPTH = 64
TILES = 8
HALO = 8
SMEM = pl.BlockSpec(memory_space=pltpu.SMEM)
VMEM = pl.BlockSpec(memory_space=pltpu.VMEM)
LIMIT = 48 * 1024 * 1024


def lane_index(rows):
    return lax.broadcasted_iota(jnp.int32, (rows, LANES), 1)


def column_lerp(plane, rel, near, far):
    rows = plane.shape[0]
    lane = lane_index(rows)
    keep_near = lane >= rel
    keep_far = lane >= rel + 1
    last_near = jnp.zeros((rows, LANES), jnp.float32)
    last_far = last_near
    out = []
    for j in range(BLOCKS):
        block = plane[:, j * LANES : (j + 1) * LANES]
        turn_near = pltpu.roll(block, rel, 1)
        turn_far = pltpu.roll(block, rel + 1, 1)
        out.append(
            near * jnp.where(keep_near, turn_near, last_near)
            + far * jnp.where(keep_far, turn_far, last_far)
        )
        last_near, last_far = turn_near, turn_far
    return out


def shift_columns(blocks, distance):
    rows = blocks[0].shape[0]
    part = distance & (LANES - 1)
    whole = jnp.full((rows, LANES), distance >> 7, jnp.int32) == 1
    own = lane_index(rows) >= part
    zero = jnp.zeros_like(blocks[0])
    turned = [pltpu.roll(block, part, 1) for block in blocks]
    placed = [jnp.where(whole, turned[j - 1] if j else zero, turned[j]) for j in range(BLOCKS)]
    return [jnp.where(own, placed[j], placed[j - 1] if j else zero) for j in range(BLOCKS)]


def column_terms(shear_ref, depth_pos, base):
    num = shear_ref[0] * depth_pos
    far = (num & 31).astype(jnp.float32) * (1.0 / 32.0)
    return (num >> 5) - base, 1.0 - far, far


def row_terms(shear_ref, depth_pos, base):
    num = shear_ref[1] * depth_pos
    far = (num & 127).astype(jnp.float32) * (1.0 / 128.0)
    return (num >> 7) - base, 1.0 - far, far


def march_rows(first, depth_idx, shear_ref, sigma, lines, stage, stage_row):
    row_base = (shear_ref[1] * depth_idx) >> 3
    total = [jnp.zeros((8, LANES), jnp.float32) for _ in range(BLOCKS)]
    light = [jnp.zeros((8, LANES), jnp.float32) for _ in range(BLOCKS)]
    trans = [jnp.ones((8, LANES), jnp.float32) for _ in range(BLOCKS)]
    for i in range(SLAB):
        rel, near, far = row_terms(shear_ref, depth_idx * SLAB + i, row_base)
        near = near * -sigma
        far = far * -sigma
        start = first + HALO - rel
        for j in range(BLOCKS):
            step = near * lines[i, j, pl.ds(start, 8), :] + far * lines[i, j, pl.ds(start - 1, 8), :]
            total[j] = total[j] + step
            after = jnp.exp2(total[j])
            light[j] = light[j] + step * (trans[j] - after)
            trans[j] = after
    col_base = (shear_ref[0] * depth_idx) >> 1
    scale = -1.0 / jnp.full((8, LANES), sigma, jnp.float32)
    total = shift_columns(total, col_base)
    light = shift_columns([scale * value for value in light], col_base)
    for j in range(BLOCKS):
        stage[pl.ds(stage_row * 16 + j, 8, stride=16), :] = total[j]
        stage[pl.ds(stage_row * 16 + 8 + j, 8, stride=16), :] = light[j]


def bulk_kernel(shear_ref, ext_ref, empty_ref, volume_ref, out_ref, lines, stage):
    depth_idx = lax.axis_index("depth")
    tile_pos = lax.axis_index("tile")
    sigma = ext_ref[0] * (4.0 / 1024.0 * math.log2(math.e))
    own_count = empty_ref[0, tile_pos]
    col_base = (shear_ref[0] * depth_idx) >> 1

    @pl.loop(0, SLAB)
    def _(i):
        rel, near, far = column_terms(shear_ref, depth_idx * SLAB + i, col_base)
        live = (i >= own_count).astype(jnp.float32)
        for c in range(ROWS // 16):
            plane = volume_ref[i, c * 16 : (c + 1) * 16, :].astype(jnp.float32)
            blocks = column_lerp(plane, rel, near * live, far * live)
            for j in range(BLOCKS):
                lines[i, j, HALO + c * 16 : HALO + (c + 1) * 16, :] = blocks[j]

    @pl.loop(1, ROWS // 8)
    def _(c):
        march_rows(c * 8, depth_idx, shear_ref, sigma, lines, stage, c * 8)

    row_base = (shear_ref[1] * depth_idx) >> 3

    @pl.loop(8, ROWS)
    def _(r):
        out_ref[(row_base + r) & (ROWS - 1)] = stage[pl.ds(r * 16, 16), :]


def edge_kernel(shear_ref, ext_ref, empty_ref, volume_ref, above_ref, bulk_ref, out_ref, lines, stage):
    depth_idx = lax.axis_index("depth")
    tile_pos = lax.axis_index("tile")
    sigma = ext_ref[0] * (4.0 / 1024.0 * math.log2(math.e))
    own_count = empty_ref[0, tile_pos]
    above_count = empty_ref[0, jnp.maximum(tile_pos - 1, 0)]
    col_base = (shear_ref[0] * depth_idx) >> 1
    row_base = (shear_ref[1] * depth_idx) >> 3
    out_ref[...] = bulk_ref[...]

    @pl.loop(0, SLAB)
    def _(i):
        rel, near, far = column_terms(shear_ref, depth_idx * SLAB + i, col_base)
        live = (i >= own_count).astype(jnp.float32)
        plane = volume_ref[i].astype(jnp.float32)[:8]
        blocks = column_lerp(plane, rel, near * live, far * live)
        live = (i >= above_count).astype(jnp.float32)
        plane = above_ref[i].astype(jnp.float32)[8:]
        halos = column_lerp(plane, rel, near * live, far * live)
        for j in range(BLOCKS):
            lines[i, j, HALO : HALO + 8, :] = blocks[j]
            lines[i, j, 0:HALO, :] = halos[j]

    march_rows(0, depth_idx, shear_ref, sigma, lines, stage, 0)
    for r in range(8):
        out_ref[(row_base + r) & (ROWS - 1)] = stage[r * 16 : (r + 1) * 16, :]


def compose_kernel(shear_ref, parts_ref, front_ref, back_ref):
    row = lax.axis_index("depth")

    def run(want_back):
        total = jnp.zeros((8, LANES), jnp.float32)
        light = jnp.zeros((8, LANES), jnp.float32)
        for d in range(DEPTH):
            is_back = ((shear_ref[1] * d) >> 3) > row
            use = jnp.where(is_back, jnp.float32(want_back), jnp.float32(1 - want_back))
            light = light + (use * jnp.exp2(total)) * parts_ref[d, 8:16, :]
            total = total + use * parts_ref[d, 0:8, :]
        return total, light

    front_ref[0:8, :], front_ref[8:16, :] = run(0)
    back_ref[0:8, :], back_ref[8:16, :] = run(1)


def spread_kernel(front_ref, back_ref, out_ref):
    total = front_ref[0:8, :] + back_ref[0:8, :]
    light = front_ref[8:16, :] + jnp.exp2(front_ref[0:8, :]) * back_ref[8:16, :]
    for p in range(DEPTH):
        out_ref[p, 0:8, :] = total
        out_ref[p, 8:16, :] = light


def image_kernel(palette_ref, whole_ref, image_ref):
    @pl.loop(0, ROWS // 8)
    def _(c):
        rows = pl.ds(pl.multiple_of(c * 8, 8), 8)
        for j in range(BLOCKS):
            columns = slice(j * LANES, (j + 1) * LANES)
            opacity = 1.0 - jnp.exp2(whole_ref[pl.ds(c * 128 + j, 8, stride=16), :])
            light = whole_ref[pl.ds(c * 128 + 8 + j, 8, stride=16), :]
            for k in range(3):
                image_ref[k, rows, columns] = palette_ref[0, k] * opacity + palette_ref[1, k] * light
            image_ref[3, rows, columns] = opacity


def call(kernel, out_shape, in_specs, scratch=()):
    return pl.pallas_call(
        kernel,
        out_shape=out_shape,
        in_specs=in_specs,
        out_specs=jax.tree.map(lambda _: VMEM, out_shape),
        scratch_shapes=list(scratch),
        compiler_params=pltpu.CompilerParams(vmem_limit_bytes=LIMIT),
    )


def per_device(volume, empty_slices, shear, extinction, palette):
    f32 = jnp.float32
    parts_shape = jax.ShapeDtypeStruct((DEPTH, 16, LANES), f32)
    piece_shape = jax.ShapeDtypeStruct((16, LANES), f32)
    down = [(i, i + 1) for i in range(TILES - 1)]
    above = lax.ppermute(volume[:, ROWS - 16 :, :], "tile", down)
    bulk = call(
        bulk_kernel,
        parts_shape,
        [SMEM, SMEM, SMEM, VMEM],
        [
            pltpu.VMEM((SLAB, BLOCKS, HALO + ROWS, LANES), f32),
            pltpu.VMEM((ROWS * 16, LANES), f32),
        ],
    )(shear, extinction, empty_slices, volume)
    parts = call(
        edge_kernel,
        parts_shape,
        [SMEM, SMEM, SMEM, VMEM, VMEM, VMEM],
        [
            pltpu.VMEM((SLAB, BLOCKS, HALO + 8, LANES), f32),
            pltpu.VMEM((8 * 16, LANES), f32),
        ],
    )(shear, extinction, empty_slices, volume[:, :16, :], above, bulk)
    parts = lax.all_to_all(parts, "depth", 0, 0, tiled=True)
    front, back = call(compose_kernel, (piece_shape, piece_shape), [SMEM, VMEM])(shear, parts)
    back = lax.ppermute(back, "tile", down)
    copies = call(spread_kernel, parts_shape, [VMEM, VMEM])(front, back)
    whole = lax.all_to_all(copies, "depth", 0, 0, tiled=True)
    image_shape = jax.ShapeDtypeStruct((4, ROWS, WIDTH), f32)
    return call(image_kernel, image_shape, [SMEM, VMEM])(palette, whole.reshape(ROWS * 16, LANES))


def solution(mesh):
    in_specs = (P("depth", "tile", None), P("depth", None), P(), P(), P())
    out_specs = P(None, "tile", None)
    return jax.shard_map(
        per_device, mesh=mesh, in_specs=in_specs, out_specs=out_specs, check_vma=False
    )
```

```python
import math

import jax
import jax.numpy as jnp
from jax import lax
from jax.experimental import pallas as pl
from jax.experimental.pallas import tpu as pltpu
from jax.sharding import PartitionSpec as P

SLAB = 16
ROWS = 64
WIDTH = 1024
LANES = 128
BLOCKS = WIDTH // LANES
DEPTH = 64
TILES = 8
HALO = 8
SMEM = pl.BlockSpec(memory_space=pltpu.SMEM)
VMEM = pl.BlockSpec(memory_space=pltpu.VMEM)
LIMIT = 48 * 1024 * 1024


TOP = 65535.0
BRICK_RANGE = (-27.0, math.log2(16 * 4 / 1024 * math.log2(math.e)) + 0.001)
IMAGE_RANGE = (-25.0, math.log2(4 * math.log2(math.e)) + 0.001)


def to_code(value):
    whole = (jnp.clip(value, 0.0, TOP) + 0.5).astype(jnp.int32)
    return whole - 32768


def from_code(code):
    return (code.astype(jnp.int32) + 32768).astype(jnp.float32)


def depth_to_code(depth, limits):
    low, high = limits
    steps = (TOP - 1.0) / (high - low)
    seen = depth >= 2.0**low
    level = (jnp.log2(jnp.where(seen, depth, 1.0)) - low) * steps + 1.0
    return to_code(jnp.where(seen, level, 0.0))


def depth_from_code(code, limits):
    low, high = limits
    level = from_code(code)
    depth = jnp.exp2((level - 1.0) * ((high - low) / (TOP - 1.0)) + low)
    return jnp.where(level > 0.5, depth, 0.0)


def encode_brick(total, light):
    depth = -total
    seen = depth >= 2.0 ** BRICK_RANGE[0]
    mean = light / (jnp.where(seen, depth, 1.0) * math.log(2.0))
    codes = [depth_to_code(depth, BRICK_RANGE), to_code(jnp.where(seen, mean * TOP, 0.0))]
    return jnp.concatenate(codes, axis=0).astype(jnp.int16)


def lane_index(rows):
    return lax.broadcasted_iota(jnp.int32, (rows, LANES), 1)


def column_lerp(plane, rel, near, far):
    rows = plane.shape[0]
    lane = lane_index(rows)
    keep_near = lane >= rel
    keep_far = lane >= rel + 1
    last_near = jnp.zeros((rows, LANES), jnp.float32)
    last_far = last_near
    out = []
    for j in range(BLOCKS):
        block = plane[:, j * LANES : (j + 1) * LANES]
        turn_near = pltpu.roll(block, rel, 1)
        turn_far = pltpu.roll(block, rel + 1, 1)
        out.append(
            near * jnp.where(keep_near, turn_near, last_near)
            + far * jnp.where(keep_far, turn_far, last_far)
        )
        last_near, last_far = turn_near, turn_far
    return out


def shift_columns(blocks, distance):
    rows = blocks[0].shape[0]
    part = distance & (LANES - 1)
    whole = jnp.full((rows, LANES), distance >> 7, jnp.int32) == 1
    own = lane_index(rows) >= part
    zero = jnp.zeros_like(blocks[0])
    turned = [pltpu.roll(block, part, 1) for block in blocks]
    placed = [jnp.where(whole, turned[j - 1] if j else zero, turned[j]) for j in range(BLOCKS)]
    return [jnp.where(own, placed[j], placed[j - 1] if j else zero) for j in range(BLOCKS)]


def column_terms(shear_ref, depth_pos, base):
    num = shear_ref[0] * depth_pos
    far = (num & 31).astype(jnp.float32) * (1.0 / 32.0)
    return (num >> 5) - base, 1.0 - far, far


def row_terms(shear_ref, depth_pos, base):
    num = shear_ref[1] * depth_pos
    far = (num & 127).astype(jnp.float32) * (1.0 / 128.0)
    return (num >> 7) - base, 1.0 - far, far


def march_rows(first, depth_idx, shear_ref, sigma, lines, stage, stage_row):
    row_base = (shear_ref[1] * depth_idx) >> 3
    total = [jnp.zeros((8, LANES), jnp.float32) for _ in range(BLOCKS)]
    light = [jnp.zeros((8, LANES), jnp.float32) for _ in range(BLOCKS)]
    trans = [jnp.ones((8, LANES), jnp.float32) for _ in range(BLOCKS)]
    for i in range(SLAB):
        rel, near, far = row_terms(shear_ref, depth_idx * SLAB + i, row_base)
        near = near * -sigma
        far = far * -sigma
        start = first + HALO - rel
        for j in range(BLOCKS):
            step = near * lines[i, j, pl.ds(start, 8), :] + far * lines[i, j, pl.ds(start - 1, 8), :]
            total[j] = total[j] + step
            after = jnp.exp2(total[j])
            light[j] = light[j] + step * (trans[j] - after)
            trans[j] = after
    col_base = (shear_ref[0] * depth_idx) >> 1
    scale = -1.0 / jnp.full((8, LANES), sigma, jnp.float32)
    total = shift_columns(total, col_base)
    light = shift_columns([scale * value for value in light], col_base)
    for j in range(BLOCKS):
        stage[pl.ds(stage_row * 16 + j, 8, stride=16), :] = total[j]
        stage[pl.ds(stage_row * 16 + 8 + j, 8, stride=16), :] = light[j]


def bulk_kernel(shear_ref, ext_ref, empty_ref, volume_ref, out_ref, lines, stage):
    depth_idx = lax.axis_index("depth")
    tile_pos = lax.axis_index("tile")
    sigma = ext_ref[0] * (4.0 / 1024.0 * math.log2(math.e))
    own_count = empty_ref[0, tile_pos]
    col_base = (shear_ref[0] * depth_idx) >> 1

    @pl.loop(0, SLAB)
    def _(i):
        rel, near, far = column_terms(shear_ref, depth_idx * SLAB + i, col_base)
        live = (i >= own_count).astype(jnp.float32)
        for c in range(ROWS // 16):
            plane = volume_ref[i, c * 16 : (c + 1) * 16, :].astype(jnp.float32)
            blocks = column_lerp(plane, rel, near * live, far * live)
            for j in range(BLOCKS):
                lines[i, j, HALO + c * 16 : HALO + (c + 1) * 16, :] = blocks[j]

    @pl.loop(1, ROWS // 8)
    def _(c):
        march_rows(c * 8, depth_idx, shear_ref, sigma, lines, stage, c * 8)

    row_base = (shear_ref[1] * depth_idx) >> 3

    @pl.loop(8, ROWS)
    def _(r):
        piece = stage[pl.ds(r * 16, 16), :]
        out_ref[(row_base + r) & (ROWS - 1)] = encode_brick(piece[:8], piece[8:])


def edge_kernel(shear_ref, ext_ref, empty_ref, volume_ref, above_ref, bulk_ref, out_ref, lines, stage):
    depth_idx = lax.axis_index("depth")
    tile_pos = lax.axis_index("tile")
    sigma = ext_ref[0] * (4.0 / 1024.0 * math.log2(math.e))
    own_count = empty_ref[0, tile_pos]
    above_count = empty_ref[0, jnp.maximum(tile_pos - 1, 0)]
    col_base = (shear_ref[0] * depth_idx) >> 1
    row_base = (shear_ref[1] * depth_idx) >> 3
    out_ref[...] = bulk_ref[...]
    above = above_ref[...].astype(jnp.float32)
    for i in range(SLAB):
        rel, near, far = column_terms(shear_ref, depth_idx * SLAB + i, col_base)
        live = (i >= own_count).astype(jnp.float32)
        plane = volume_ref[i, :16, :].astype(jnp.float32)[:8]
        blocks = column_lerp(plane, rel, near * live, far * live)
        live = (i >= above_count).astype(jnp.float32)
        halos = column_lerp(above[2 * i : 2 * i + 2], rel, near * live, far * live)
        for j in range(BLOCKS):
            lines[i, j, HALO : HALO + 8, :] = blocks[j]
            lines[i, j, HALO - 2 : HALO, :] = halos[j]

    march_rows(0, depth_idx, shear_ref, sigma, lines, stage, 0)
    for r in range(8):
        piece = stage[r * 16 : (r + 1) * 16, :]
        out_ref[(row_base + r) & (ROWS - 1)] = encode_brick(piece[:8], piece[8:])


def compose_kernel(shear_ref, parts_ref, front_ref, back_ref):
    row = lax.axis_index("depth")
    zero = jnp.zeros((8, LANES), jnp.float32)
    totals = [zero, zero]
    lights = [zero, zero]
    for d in range(DEPTH):
        codes = parts_ref[d].astype(jnp.int32)
        depth = depth_from_code(codes[:8], BRICK_RANGE)
        light = from_code(codes[8:]) * (math.log(2.0) / TOP) * depth
        is_back = (((shear_ref[1] * d) >> 3) > row).astype(jnp.float32)
        for side, use in enumerate((1.0 - is_back, is_back)):
            lights[side] = lights[side] + (use * jnp.exp2(-totals[side])) * light
            totals[side] = totals[side] + use * depth
    front_ref[0:8, :], front_ref[8:16, :] = totals[0], lights[0]
    back_ref[0:8, :], back_ref[8:16, :] = totals[1], lights[1]


def spread_kernel(front_ref, back_ref, out_ref):
    depth = front_ref[0:8, :] + back_ref[0:8, :]
    light = front_ref[8:16, :] + jnp.exp2(-front_ref[0:8, :]) * back_ref[8:16, :]
    opacity = 1.0 - jnp.exp2(-depth)
    mean = light / jnp.maximum(opacity, 2.0 ** IMAGE_RANGE[0])
    codes = jnp.concatenate([depth_to_code(depth, IMAGE_RANGE), to_code(mean * TOP)], axis=0)
    codes = codes.astype(jnp.int16)
    for p in range(DEPTH):
        out_ref[p] = codes


def image_kernel(palette_ref, whole_ref, image_ref, stage):
    @pl.loop(0, ROWS // 8)
    def _(c):
        for r in range(8):
            codes = whole_ref[c * 8 + r].astype(jnp.int32)
            opacity = 1.0 - jnp.exp2(-depth_from_code(codes[:8], IMAGE_RANGE))
            stage[r * 16 : r * 16 + 8, :] = opacity
            stage[r * 16 + 8 : r * 16 + 16, :] = from_code(codes[8:]) * (1.0 / TOP) * opacity
        rows = pl.ds(pl.multiple_of(c * 8, 8), 8)
        for j in range(BLOCKS):
            columns = slice(j * LANES, (j + 1) * LANES)
            opacity = stage[pl.ds(j, 8, stride=16), :]
            light = stage[pl.ds(8 + j, 8, stride=16), :]
            for k in range(3):
                image_ref[k, rows, columns] = palette_ref[0, k] * opacity + palette_ref[1, k] * light
            image_ref[3, rows, columns] = opacity


def call(kernel, out_shape, in_specs, scratch=()):
    return pl.pallas_call(
        kernel,
        out_shape=out_shape,
        in_specs=in_specs,
        out_specs=jax.tree.map(lambda _: VMEM, out_shape),
        scratch_shapes=list(scratch),
        compiler_params=pltpu.CompilerParams(vmem_limit_bytes=LIMIT),
    )


def per_device(volume, empty_slices, shear, extinction, palette):
    f32 = jnp.float32
    parts_shape = jax.ShapeDtypeStruct((DEPTH, 16, LANES), jnp.int16)
    piece_shape = jax.ShapeDtypeStruct((16, LANES), f32)
    down = [(i, i + 1) for i in range(TILES - 1)]
    above = lax.ppermute(volume[:, ROWS - 2 :, :].reshape(2 * SLAB, WIDTH), "tile", down)
    bulk = call(
        bulk_kernel,
        parts_shape,
        [SMEM, SMEM, SMEM, VMEM],
        [
            pltpu.VMEM((SLAB, BLOCKS, HALO + ROWS, LANES), f32),
            pltpu.VMEM((ROWS * 16, LANES), f32),
        ],
    )(shear, extinction, empty_slices, volume)
    parts = call(
        edge_kernel,
        parts_shape,
        [SMEM, SMEM, SMEM, VMEM, VMEM, VMEM],
        [
            pltpu.VMEM((SLAB, BLOCKS, HALO + 8, LANES), f32),
            pltpu.VMEM((8 * 16, LANES), f32),
        ],
    )(shear, extinction, empty_slices, volume, above, bulk)
    parts = lax.all_to_all(parts, "depth", 0, 0, tiled=True)
    front, back = call(compose_kernel, (piece_shape, piece_shape), [SMEM, VMEM])(shear, parts)
    back = lax.ppermute(back, "tile", down)
    copies = call(spread_kernel, parts_shape, [VMEM, VMEM])(front, back)
    whole = lax.all_to_all(copies, "depth", 0, 0, tiled=True)
    image_shape = jax.ShapeDtypeStruct((4, ROWS, WIDTH), f32)
    return call(image_kernel, image_shape, [SMEM, VMEM], [pltpu.VMEM((8 * 16, LANES), f32)])(
        palette, whole
    )


def solution(mesh):
    in_specs = (P("depth", "tile", None), P("depth", None), P(), P(), P())
    out_specs = P(None, "tile", None)
    return jax.shard_map(
        per_device, mesh=mesh, in_specs=in_specs, out_specs=out_specs, check_vma=False
    )
```

```python
import math

import jax
import jax.numpy as jnp
from jax import lax
from jax.experimental import pallas as pl
from jax.experimental.pallas import tpu as pltpu
from jax.sharding import PartitionSpec as P

SLAB = 16
ROWS = 64
WIDTH = 1024
LANES = 128
BLOCKS = WIDTH // LANES
DEPTH = 64
TILES = 8
HALO = 8
SMEM = pl.BlockSpec(memory_space=pltpu.SMEM)
VMEM = pl.BlockSpec(memory_space=pltpu.VMEM)
LIMIT = 48 * 1024 * 1024


TOP = 65535.0
BRICK_RANGE = (-27.0, math.log2(16 * 4 / 1024 * math.log2(math.e)) + 0.001)
IMAGE_RANGE = (-25.0, math.log2(4 * math.log2(math.e)) + 0.001)


def to_code(value):
    whole = (jnp.clip(value, 0.0, TOP) + 0.5).astype(jnp.int32)
    return whole - 32768


def from_code(code):
    return (code.astype(jnp.int32) + 32768).astype(jnp.float32)


def depth_to_code(depth, limits):
    low, high = limits
    steps = (TOP - 1.0) / (high - low)
    seen = depth >= 2.0**low
    level = (jnp.log2(jnp.where(seen, depth, 1.0)) - low) * steps + 1.0
    return to_code(jnp.where(seen, level, 0.0))


def depth_from_code(code, limits):
    low, high = limits
    level = from_code(code)
    depth = jnp.exp2((level - 1.0) * ((high - low) / (TOP - 1.0)) + low)
    return jnp.where(level > 0.5, depth, 0.0)


def encode_brick(total, light):
    depth = -total
    seen = depth >= 2.0 ** BRICK_RANGE[0]
    mean = light / (jnp.where(seen, depth, 1.0) * math.log(2.0))
    codes = [depth_to_code(depth, BRICK_RANGE), to_code(jnp.where(seen, mean * TOP, 0.0))]
    return jnp.concatenate(codes, axis=0).astype(jnp.int16)


def lane_index(rows):
    return lax.broadcasted_iota(jnp.int32, (rows, LANES), 1)


def column_lerp(plane, rel, near, far):
    rows = plane.shape[0]
    lane = lane_index(rows)
    keep_near = lane >= rel
    keep_far = lane >= rel + 1
    last_near = jnp.zeros((rows, LANES), jnp.float32)
    last_far = last_near
    out = []
    for j in range(BLOCKS):
        block = plane[:, j * LANES : (j + 1) * LANES]
        turn_near = pltpu.roll(block, rel, 1)
        turn_far = pltpu.roll(block, rel + 1, 1)
        out.append(
            near * jnp.where(keep_near, turn_near, last_near)
            + far * jnp.where(keep_far, turn_far, last_far)
        )
        last_near, last_far = turn_near, turn_far
    return out


def shift_columns(blocks, distance):
    rows = blocks[0].shape[0]
    part = distance & (LANES - 1)
    whole = jnp.full((rows, LANES), distance >> 7, jnp.int32) == 1
    own = lane_index(rows) >= part
    zero = jnp.zeros_like(blocks[0])
    turned = [pltpu.roll(block, part, 1) for block in blocks]
    placed = [jnp.where(whole, turned[j - 1] if j else zero, turned[j]) for j in range(BLOCKS)]
    return [jnp.where(own, placed[j], placed[j - 1] if j else zero) for j in range(BLOCKS)]


def column_terms(shear_ref, depth_pos, base):
    num = shear_ref[0] * depth_pos
    far = (num & 31).astype(jnp.float32) * (1.0 / 32.0)
    return (num >> 5) - base, 1.0 - far, far


def row_terms(shear_ref, depth_pos, base):
    num = shear_ref[1] * depth_pos
    far = (num & 127).astype(jnp.float32) * (1.0 / 128.0)
    return (num >> 7) - base, 1.0 - far, far


def march_rows(first, depth_idx, shear_ref, sigma, lines, stage, stage_row):
    row_base = (shear_ref[1] * depth_idx) >> 3
    total = [jnp.zeros((8, LANES), jnp.float32) for _ in range(BLOCKS)]
    light = [jnp.zeros((8, LANES), jnp.float32) for _ in range(BLOCKS)]
    trans = [jnp.ones((8, LANES), jnp.float32) for _ in range(BLOCKS)]
    for i in range(SLAB):
        rel, near, far = row_terms(shear_ref, depth_idx * SLAB + i, row_base)
        near = near * -sigma
        far = far * -sigma
        start = first + HALO - rel
        for j in range(BLOCKS):
            step = near * lines[i, j, pl.ds(start, 8), :] + far * lines[i, j, pl.ds(start - 1, 8), :]
            total[j] = total[j] + step
            after = jnp.exp2(total[j])
            light[j] = light[j] + step * (trans[j] - after)
            trans[j] = after
    col_base = (shear_ref[0] * depth_idx) >> 1
    scale = -1.0 / jnp.full((8, LANES), sigma, jnp.float32)
    total = shift_columns(total, col_base)
    light = shift_columns([scale * value for value in light], col_base)
    for j in range(BLOCKS):
        stage[pl.ds(stage_row * 16 + j, 8, stride=16), :] = total[j]
        stage[pl.ds(stage_row * 16 + 8 + j, 8, stride=16), :] = light[j]


def bulk_kernel(shear_ref, ext_ref, empty_ref, volume_ref, out_ref, lines, stage):
    depth_idx = lax.axis_index("depth")
    tile_pos = lax.axis_index("tile")
    sigma = ext_ref[0] * (4.0 / 1024.0 * math.log2(math.e))
    own_count = empty_ref[0, tile_pos]
    col_base = (shear_ref[0] * depth_idx) >> 1

    @pl.loop(0, SLAB)
    def _(i):
        rel, near, far = column_terms(shear_ref, depth_idx * SLAB + i, col_base)
        live = (i >= own_count).astype(jnp.float32)
        for c in range(ROWS // 16):
            plane = volume_ref[i, c * 16 : (c + 1) * 16, :].astype(jnp.float32)
            blocks = column_lerp(plane, rel, near * live, far * live)
            for j in range(BLOCKS):
                lines[i, j, HALO + c * 16 : HALO + (c + 1) * 16, :] = blocks[j]

    @pl.loop(1, ROWS // 8)
    def _(c):
        march_rows(c * 8, depth_idx, shear_ref, sigma, lines, stage, c * 8)

    row_base = (shear_ref[1] * depth_idx) >> 3

    @pl.loop(8, ROWS, step=8)
    def _(first):
        for r in range(8):
            piece = stage[pl.ds((first + r) * 16, 16), :]
            out_ref[(row_base + first + r) & (ROWS - 1)] = encode_brick(piece[:8], piece[8:])


def edge_kernel(shear_ref, ext_ref, empty_ref, volume_ref, above_ref, bulk_ref, out_ref, lines, stage):
    depth_idx = lax.axis_index("depth")
    tile_pos = lax.axis_index("tile")
    sigma = ext_ref[0] * (4.0 / 1024.0 * math.log2(math.e))
    own_count = empty_ref[0, tile_pos]
    above_count = empty_ref[0, jnp.maximum(tile_pos - 1, 0)]
    col_base = (shear_ref[0] * depth_idx) >> 1
    row_base = (shear_ref[1] * depth_idx) >> 3
    out_ref[...] = bulk_ref[...]
    above = above_ref[...].astype(jnp.float32)
    for i in range(SLAB):
        rel, near, far = column_terms(shear_ref, depth_idx * SLAB + i, col_base)
        live = (i >= own_count).astype(jnp.float32)
        plane = volume_ref[i].astype(jnp.float32)[:8]
        blocks = column_lerp(plane, rel, near * live, far * live)
        live = (i >= above_count).astype(jnp.float32)
        halos = column_lerp(above[2 * i : 2 * i + 2], rel, near * live, far * live)
        for j in range(BLOCKS):
            lines[i, j, HALO : HALO + 8, :] = blocks[j]
            lines[i, j, HALO - 2 : HALO, :] = halos[j]

    march_rows(0, depth_idx, shear_ref, sigma, lines, stage, 0)
    for r in range(8):
        piece = stage[r * 16 : (r + 1) * 16, :]
        out_ref[(row_base + r) & (ROWS - 1)] = encode_brick(piece[:8], piece[8:])


def compose_kernel(shear_ref, parts_ref, front_ref, back_ref):
    row = lax.axis_index("depth")
    zero = jnp.zeros((8, LANES), jnp.float32)
    totals = [zero, zero]
    lights = [zero, zero]
    for d in range(DEPTH):
        codes = parts_ref[d].astype(jnp.int32)
        depth = depth_from_code(codes[:8], BRICK_RANGE)
        light = from_code(codes[8:]) * (math.log(2.0) / TOP) * depth
        is_back = (((shear_ref[1] * d) >> 3) > row).astype(jnp.float32)
        for side, use in enumerate((1.0 - is_back, is_back)):
            lights[side] = lights[side] + (use * jnp.exp2(-totals[side])) * light
            totals[side] = totals[side] + use * depth
    front_ref[0:8, :], front_ref[8:16, :] = totals[0], lights[0]
    back_ref[0:8, :], back_ref[8:16, :] = totals[1], lights[1]


def spread_kernel(front_ref, back_ref, out_ref):
    depth = front_ref[0:8, :] + back_ref[0:8, :]
    light = front_ref[8:16, :] + jnp.exp2(-front_ref[0:8, :]) * back_ref[8:16, :]
    opacity = 1.0 - jnp.exp2(-depth)
    mean = light / jnp.maximum(opacity, 2.0 ** IMAGE_RANGE[0])
    codes = jnp.concatenate([depth_to_code(depth, IMAGE_RANGE), to_code(mean * TOP)], axis=0)
    codes = codes.astype(jnp.int16)
    for p in range(DEPTH):
        out_ref[p] = codes


def image_kernel(palette_ref, whole_ref, image_hbm, stage, image, sems):
    base = [palette_ref[0, k] for k in range(3)]
    slope = [palette_ref[1, k] for k in range(3)]
    copies = []
    for c in range(ROWS // 8):
        rows = slice(c * 8, (c + 1) * 8)
        for r in range(c * 8, c * 8 + 8):
            codes = whole_ref[r].astype(jnp.int32)
            opacity = 1.0 - jnp.exp2(-depth_from_code(codes[:8], IMAGE_RANGE))
            stage[r * 16 : r * 16 + 8, :] = opacity
            stage[r * 16 + 8 : r * 16 + 16, :] = from_code(codes[8:]) * (1.0 / TOP) * opacity
        for j in range(BLOCKS):
            columns = slice(j * LANES, (j + 1) * LANES)
            opacity = stage[pl.ds(c * 128 + j, 8, stride=16), :]
            light = stage[pl.ds(c * 128 + 8 + j, 8, stride=16), :]
            for k in range(3):
                image[k, rows, columns] = base[k] * opacity + slope[k] * light
            image[3, rows, columns] = opacity
        if c % 2:
            part = pl.ds(c * 8 - 8, 16)
            copies.append(
                pltpu.make_async_copy(image.at[:, part], image_hbm.at[:, part], sems.at[c // 2])
            )
            copies[-1].start()
    for copy in copies:
        copy.wait()


def call(kernel, out_shape, in_specs, scratch=(), out_specs=None):
    return pl.pallas_call(
        kernel,
        out_shape=out_shape,
        in_specs=in_specs,
        out_specs=out_specs or jax.tree.map(lambda _: VMEM, out_shape),
        scratch_shapes=list(scratch),
        compiler_params=pltpu.CompilerParams(vmem_limit_bytes=LIMIT),
    )


def per_device(volume, empty_slices, shear, extinction, palette):
    f32 = jnp.float32
    parts_shape = jax.ShapeDtypeStruct((DEPTH, 16, LANES), jnp.int16)
    piece_shape = jax.ShapeDtypeStruct((16, LANES), f32)
    down = [(i, i + 1) for i in range(TILES - 1)]
    first, last = lax.optimization_barrier((volume[:, :16, :], volume[:, ROWS - 16 :, :]))
    above = lax.ppermute(last[:, 14:, :].reshape(2 * SLAB, WIDTH), "tile", down)
    bulk = call(
        bulk_kernel,
        parts_shape,
        [SMEM, SMEM, SMEM, VMEM],
        [
            pltpu.VMEM((SLAB, BLOCKS, HALO + ROWS, LANES), f32),
            pltpu.VMEM((ROWS * 16, LANES), f32),
        ],
    )(shear, extinction, empty_slices, volume)
    parts = call(
        edge_kernel,
        parts_shape,
        [SMEM, SMEM, SMEM, VMEM, VMEM, VMEM],
        [
            pltpu.VMEM((SLAB, BLOCKS, HALO + 8, LANES), f32),
            pltpu.VMEM((8 * 16, LANES), f32),
        ],
    )(shear, extinction, empty_slices, first, above, bulk)
    parts = lax.all_to_all(parts, "depth", 0, 0, tiled=True)
    front, back = call(compose_kernel, (piece_shape, piece_shape), [SMEM, VMEM])(shear, parts)
    back = lax.ppermute(back, "tile", down)
    copies = call(spread_kernel, parts_shape, [VMEM, VMEM])(front, back)
    whole = lax.all_to_all(copies, "depth", 0, 0, tiled=True)
    image_shape = jax.ShapeDtypeStruct((4, ROWS, WIDTH), f32)
    return call(
        image_kernel,
        image_shape,
        [SMEM, VMEM],
        [
            pltpu.VMEM((ROWS * 16, LANES), f32),
            pltpu.VMEM((4, ROWS, WIDTH), f32),
            pltpu.SemaphoreType.DMA((ROWS // 16,)),
        ],
        pl.BlockSpec(memory_space=pl.ANY),
    )(palette, whole)


def solution(mesh):
    in_specs = (P("depth", "tile", None), P("depth", None), P(), P(), P())
    out_specs = P(None, "tile", None)
    return jax.shard_map(
        per_device, mesh=mesh, in_specs=in_specs, out_specs=out_specs, check_vma=False
    )
```

```python
import math

import jax
import jax.numpy as jnp
from jax import lax
from jax.experimental import pallas as pl
from jax.experimental.pallas import tpu as pltpu
from jax.sharding import PartitionSpec as P

SLAB = 16
ROWS = 64
WIDTH = 1024
LANES = 128
BLOCKS = WIDTH // LANES
DEPTH = 64
TILES = 8
HALO = 8
SMEM = pl.BlockSpec(memory_space=pltpu.SMEM)
VMEM = pl.BlockSpec(memory_space=pltpu.VMEM)
LIMIT = 48 * 1024 * 1024


TOP = 65535.0
BRICK_RANGE = (-27.0, math.log2(16 * 4 / 1024 * math.log2(math.e)) + 0.001)
IMAGE_RANGE = (-25.0, math.log2(4 * math.log2(math.e)) + 0.001)


def to_code(value):
    whole = (jnp.clip(value, 0.0, TOP) + 0.5).astype(jnp.int32)
    return whole - 32768


def from_code(code):
    return (code.astype(jnp.int32) + 32768).astype(jnp.float32)


def depth_to_code(depth, limits):
    low, high = limits
    steps = (TOP - 1.0) / (high - low)
    seen = depth >= 2.0**low
    level = (jnp.log2(jnp.where(seen, depth, 1.0)) - low) * steps + 1.0
    return to_code(jnp.where(seen, level, 0.0))


def depth_from_code(code, limits):
    low, high = limits
    level = from_code(code)
    depth = jnp.exp2((level - 1.0) * ((high - low) / (TOP - 1.0)) + low)
    return jnp.where(level > 0.5, depth, 0.0)


def encode_brick(total, light):
    depth = -total
    seen = depth >= 2.0 ** BRICK_RANGE[0]
    mean = light / (jnp.where(seen, depth, 1.0) * math.log(2.0))
    codes = [depth_to_code(depth, BRICK_RANGE), to_code(jnp.where(seen, mean * TOP, 0.0))]
    return jnp.concatenate(codes, axis=0).astype(jnp.int16)


def lane_index(rows):
    return lax.broadcasted_iota(jnp.int32, (rows, LANES), 1)


def column_lerp(plane, rel, near, far):
    rows = plane.shape[0]
    lane = lane_index(rows)
    keep_near = lane >= rel
    keep_far = lane >= rel + 1
    last_near = jnp.zeros((rows, LANES), jnp.float32)
    last_far = last_near
    out = []
    for j in range(BLOCKS):
        block = plane[:, j * LANES : (j + 1) * LANES]
        turn_near = pltpu.roll(block, rel, 1)
        turn_far = pltpu.roll(block, rel + 1, 1)
        out.append(
            near * jnp.where(keep_near, turn_near, last_near)
            + far * jnp.where(keep_far, turn_far, last_far)
        )
        last_near, last_far = turn_near, turn_far
    return out


def shift_columns(blocks, distance):
    rows = blocks[0].shape[0]
    part = distance & (LANES - 1)
    whole = jnp.full((rows, LANES), distance >> 7, jnp.int32) == 1
    own = lane_index(rows) >= part
    zero = jnp.zeros_like(blocks[0])
    turned = [pltpu.roll(block, part, 1) for block in blocks]
    placed = [jnp.where(whole, turned[j - 1] if j else zero, turned[j]) for j in range(BLOCKS)]
    return [jnp.where(own, placed[j], placed[j - 1] if j else zero) for j in range(BLOCKS)]


def column_terms(shear_ref, depth_pos, base):
    num = shear_ref[0] * depth_pos
    far = (num & 31).astype(jnp.float32) * (1.0 / 32.0)
    return (num >> 5) - base, 1.0 - far, far


def row_terms(shear_ref, depth_pos, base):
    num = shear_ref[1] * depth_pos
    far = (num & 127).astype(jnp.float32) * (1.0 / 128.0)
    return (num >> 7) - base, 1.0 - far, far


def march_rows(first, depth_idx, shear_ref, sigma, lines, stage, stage_row):
    row_base = (shear_ref[1] * depth_idx) >> 3
    total = [jnp.zeros((8, LANES), jnp.float32) for _ in range(BLOCKS)]
    light = [jnp.zeros((8, LANES), jnp.float32) for _ in range(BLOCKS)]
    trans = [jnp.ones((8, LANES), jnp.float32) for _ in range(BLOCKS)]
    for i in range(SLAB):
        rel, near, far = row_terms(shear_ref, depth_idx * SLAB + i, row_base)
        near = near * -sigma
        far = far * -sigma
        start = first + HALO - rel
        for j in range(BLOCKS):
            step = near * lines[i, j, pl.ds(start, 8), :] + far * lines[i, j, pl.ds(start - 1, 8), :]
            total[j] = total[j] + step
            after = jnp.exp2(total[j])
            light[j] = light[j] + step * (trans[j] - after)
            trans[j] = after
    col_base = (shear_ref[0] * depth_idx) >> 1
    scale = -1.0 / jnp.full((8, LANES), sigma, jnp.float32)
    total = shift_columns(total, col_base)
    light = shift_columns([scale * value for value in light], col_base)
    for j in range(BLOCKS):
        stage[pl.ds(stage_row * 16 + j, 8, stride=16), :] = total[j]
        stage[pl.ds(stage_row * 16 + 8 + j, 8, stride=16), :] = light[j]


def bulk_kernel(shear_ref, ext_ref, empty_ref, volume_ref, out_ref, lines, stage):
    depth_idx = lax.axis_index("depth")
    tile_pos = lax.axis_index("tile")
    sigma = ext_ref[0] * (4.0 / 1024.0 * math.log2(math.e))
    own_count = empty_ref[0, tile_pos]
    col_base = (shear_ref[0] * depth_idx) >> 1

    @pl.loop(0, SLAB, unroll=SLAB)
    def _(i):
        rel, near, far = column_terms(shear_ref, depth_idx * SLAB + i, col_base)
        live = (i >= own_count).astype(jnp.float32)
        for c in range(ROWS // 16):
            plane = volume_ref[i, c * 16 : (c + 1) * 16, :].astype(jnp.float32)
            blocks = column_lerp(plane, rel, near * live, far * live)
            for j in range(BLOCKS):
                lines[i, j, HALO + c * 16 : HALO + (c + 1) * 16, :] = blocks[j]

    @pl.loop(1, ROWS // 8, unroll=ROWS // 8 - 1)
    def _(c):
        march_rows(c * 8, depth_idx, shear_ref, sigma, lines, stage, c * 8)

    row_base = (shear_ref[1] * depth_idx) >> 3

    @pl.loop(8, ROWS, step=8, unroll=ROWS // 8 - 1)
    def _(first):
        for r in range(8):
            piece = stage[pl.ds((first + r) * 16, 16), :]
            out_ref[(row_base + first + r) & (ROWS - 1)] = encode_brick(piece[:8], piece[8:])


def edge_kernel(shear_ref, ext_ref, empty_ref, volume_ref, above_ref, bulk_ref, out_ref, lines, stage):
    depth_idx = lax.axis_index("depth")
    tile_pos = lax.axis_index("tile")
    sigma = ext_ref[0] * (4.0 / 1024.0 * math.log2(math.e))
    own_count = empty_ref[0, tile_pos]
    above_count = empty_ref[0, jnp.maximum(tile_pos - 1, 0)]
    col_base = (shear_ref[0] * depth_idx) >> 1
    row_base = (shear_ref[1] * depth_idx) >> 3
    out_ref[...] = bulk_ref[...]
    above = above_ref[...].astype(jnp.float32)
    for i in range(SLAB):
        rel, near, far = column_terms(shear_ref, depth_idx * SLAB + i, col_base)
        live = (i >= own_count).astype(jnp.float32)
        plane = volume_ref[i].astype(jnp.float32)[:8]
        blocks = column_lerp(plane, rel, near * live, far * live)
        live = (i >= above_count).astype(jnp.float32)
        halos = column_lerp(above[2 * i : 2 * i + 2], rel, near * live, far * live)
        for j in range(BLOCKS):
            lines[i, j, HALO : HALO + 8, :] = blocks[j]
            lines[i, j, HALO - 2 : HALO, :] = halos[j]

    march_rows(0, depth_idx, shear_ref, sigma, lines, stage, 0)
    for r in range(8):
        piece = stage[r * 16 : (r + 1) * 16, :]
        out_ref[(row_base + r) & (ROWS - 1)] = encode_brick(piece[:8], piece[8:])


def compose_kernel(shear_ref, parts_ref, front_ref, back_ref):
    limit = jnp.full((8, LANES), 8 * lax.axis_index("depth") + 8, jnp.int32)
    slope = jnp.full((8, LANES), shear_ref[1], jnp.int32)
    zero = jnp.zeros((8, LANES), jnp.float32)
    reach = jnp.zeros((8, LANES), jnp.int32)
    total, front_total, front_light, back_light = zero, zero, zero, zero
    for d in range(DEPTH):
        codes = parts_ref[d].astype(jnp.int32)
        depth = depth_from_code(codes[:8], BRICK_RANGE)
        light = from_code(codes[8:]) * depth * jnp.exp2(-total)
        in_front = reach < limit
        front_total = jnp.where(in_front, front_total + depth, front_total)
        front_light = jnp.where(in_front, front_light + light, front_light)
        back_light = jnp.where(in_front, back_light, back_light + light)
        total = total + depth
        reach = reach + slope
    scale = math.log(2.0) / TOP
    front_ref[0:8, :] = front_total
    front_ref[8:16, :] = front_light * scale
    back_ref[0:8, :] = total - front_total
    back_ref[8:16, :] = back_light * scale * jnp.exp2(front_total)


def spread_kernel(front_ref, back_ref, out_ref):
    depth = front_ref[0:8, :] + back_ref[0:8, :]
    light = front_ref[8:16, :] + jnp.exp2(-front_ref[0:8, :]) * back_ref[8:16, :]
    opacity = 1.0 - jnp.exp2(-depth)
    mean = light / jnp.maximum(opacity, 2.0 ** IMAGE_RANGE[0])
    codes = jnp.concatenate([depth_to_code(depth, IMAGE_RANGE), to_code(mean * TOP)], axis=0)
    codes = codes.astype(jnp.int16)
    for p in range(DEPTH):
        out_ref[p] = codes


def image_kernel(palette_ref, whole_ref, image_hbm, stage, image, sems):
    base = [palette_ref[0, k] for k in range(3)]
    slope = [palette_ref[1, k] for k in range(3)]
    copies = []
    for c in range(ROWS // 8):
        rows = slice(c * 8, (c + 1) * 8)
        for r in range(c * 8, c * 8 + 8):
            codes = whole_ref[r].astype(jnp.int32)
            opacity = 1.0 - jnp.exp2(-depth_from_code(codes[:8], IMAGE_RANGE))
            stage[r * 16 : r * 16 + 8, :] = opacity
            stage[r * 16 + 8 : r * 16 + 16, :] = from_code(codes[8:]) * (1.0 / TOP) * opacity
        for j in range(BLOCKS):
            columns = slice(j * LANES, (j + 1) * LANES)
            opacity = stage[pl.ds(c * 128 + j, 8, stride=16), :]
            light = stage[pl.ds(c * 128 + 8 + j, 8, stride=16), :]
            for k in range(3):
                image[k, rows, columns] = base[k] * opacity + slope[k] * light
            image[3, rows, columns] = opacity
        if c % 2:
            part = pl.ds(c * 8 - 8, 16)
            copies.append(
                pltpu.make_async_copy(image.at[:, part], image_hbm.at[:, part], sems.at[c // 2])
            )
            copies[-1].start()
    for copy in copies:
        copy.wait()


def call(kernel, out_shape, in_specs, scratch=(), out_specs=None):
    return pl.pallas_call(
        kernel,
        out_shape=out_shape,
        in_specs=in_specs,
        out_specs=out_specs or jax.tree.map(lambda _: VMEM, out_shape),
        scratch_shapes=list(scratch),
        compiler_params=pltpu.CompilerParams(vmem_limit_bytes=LIMIT),
    )


def per_device(volume, empty_slices, shear, extinction, palette):
    f32 = jnp.float32
    parts_shape = jax.ShapeDtypeStruct((DEPTH, 16, LANES), jnp.int16)
    piece_shape = jax.ShapeDtypeStruct((16, LANES), f32)
    down = [(i, i + 1) for i in range(TILES - 1)]
    first, last = lax.optimization_barrier((volume[:, :16, :], volume[:, ROWS - 16 :, :]))
    above = lax.ppermute(last[:, 14:, :].reshape(2 * SLAB, WIDTH), "tile", down)
    bulk = call(
        bulk_kernel,
        parts_shape,
        [SMEM, SMEM, SMEM, VMEM],
        [
            pltpu.VMEM((SLAB, BLOCKS, HALO + ROWS, LANES), f32),
            pltpu.VMEM((ROWS * 16, LANES), f32),
        ],
    )(shear, extinction, empty_slices, volume)
    parts = call(
        edge_kernel,
        parts_shape,
        [SMEM, SMEM, SMEM, VMEM, VMEM, VMEM],
        [
            pltpu.VMEM((SLAB, BLOCKS, HALO + 8, LANES), f32),
            pltpu.VMEM((8 * 16, LANES), f32),
        ],
    )(shear, extinction, empty_slices, first, above, bulk)
    parts = lax.all_to_all(parts, "depth", 0, 0, tiled=True)
    front, back = call(compose_kernel, (piece_shape, piece_shape), [SMEM, VMEM])(shear, parts)
    back = lax.ppermute(back, "tile", down)
    copies = call(spread_kernel, parts_shape, [VMEM, VMEM])(front, back)
    whole = lax.all_to_all(copies, "depth", 0, 0, tiled=True)
    image_shape = jax.ShapeDtypeStruct((4, ROWS, WIDTH), f32)
    return call(
        image_kernel,
        image_shape,
        [SMEM, VMEM],
        [
            pltpu.VMEM((ROWS * 16, LANES), f32),
            pltpu.VMEM((4, ROWS, WIDTH), f32),
            pltpu.SemaphoreType.DMA((ROWS // 16,)),
        ],
        pl.BlockSpec(memory_space=pl.ANY),
    )(palette, whole)


def solution(mesh):
    in_specs = (P("depth", "tile", None), P("depth", None), P(), P(), P())
    out_specs = P(None, "tile", None)
    return jax.shard_map(
        per_device, mesh=mesh, in_specs=in_specs, out_specs=out_specs, check_vma=False
    )
```

```python
import math

import jax
import jax.numpy as jnp
from jax import lax
from jax.experimental import pallas as pl
from jax.experimental.pallas import tpu as pltpu
from jax.sharding import PartitionSpec as P

SLAB = 16
ROWS = 64
WIDTH = 1024
LANES = 128
BLOCKS = WIDTH // LANES
DEPTH = 64
TILES = 8
HALO = 8
SMEM = pl.BlockSpec(memory_space=pltpu.SMEM)
VMEM = pl.BlockSpec(memory_space=pltpu.VMEM)
LIMIT = 48 * 1024 * 1024


TOP = 65535.0
BRICK_RANGE = (-27.0, math.log2(16 * 4 / 1024 * math.log2(math.e)) + 0.001)
IMAGE_RANGE = (-25.0, math.log2(4 * math.log2(math.e)) + 0.001)


def to_code(value):
    whole = (jnp.clip(value, 0.0, TOP) + 0.5).astype(jnp.int32)
    return whole - 32768


def from_code(code):
    return (code.astype(jnp.int32) + 32768).astype(jnp.float32)


def depth_to_code(depth, limits):
    low, high = limits
    steps = (TOP - 1.0) / (high - low)
    seen = depth >= 2.0**low
    level = (jnp.log2(jnp.where(seen, depth, 1.0)) - low) * steps + 1.0
    return to_code(jnp.where(seen, level, 0.0))


def depth_from_code(code, limits):
    low, high = limits
    level = from_code(code)
    depth = jnp.exp2((level - 1.0) * ((high - low) / (TOP - 1.0)) + low)
    return jnp.where(level > 0.5, depth, 0.0)


def encode_brick(total, light):
    depth = -total
    seen = depth >= 2.0 ** BRICK_RANGE[0]
    mean = light / (jnp.where(seen, depth, 1.0) * math.log(2.0))
    codes = [depth_to_code(depth, BRICK_RANGE), to_code(jnp.where(seen, mean * TOP, 0.0))]
    return jnp.concatenate(codes, axis=0).astype(jnp.int16)


def lane_index(rows):
    return lax.broadcasted_iota(jnp.int32, (rows, LANES), 1)


def column_lerp(plane, rel, near, far):
    rows = plane.shape[0]
    lane = lane_index(rows)
    keep_near = lane >= rel
    keep_far = lane >= rel + 1
    last_near = jnp.zeros((rows, LANES), jnp.float32)
    last_far = last_near
    out = []
    for j in range(BLOCKS):
        block = plane[:, j * LANES : (j + 1) * LANES]
        turn_near = pltpu.roll(block, rel, 1)
        turn_far = pltpu.roll(block, rel + 1, 1)
        out.append(
            near * jnp.where(keep_near, turn_near, last_near)
            + far * jnp.where(keep_far, turn_far, last_far)
        )
        last_near, last_far = turn_near, turn_far
    return out


def shift_columns(blocks, distance):
    rows = blocks[0].shape[0]
    part = distance & (LANES - 1)
    whole = jnp.full((rows, LANES), distance >> 7, jnp.int32) == 1
    own = lane_index(rows) >= part
    zero = jnp.zeros_like(blocks[0])
    turned = [pltpu.roll(block, part, 1) for block in blocks]
    placed = [jnp.where(whole, turned[j - 1] if j else zero, turned[j]) for j in range(BLOCKS)]
    return [jnp.where(own, placed[j], placed[j - 1] if j else zero) for j in range(BLOCKS)]


def column_terms(shear_ref, depth_pos, base):
    num = shear_ref[0] * depth_pos
    far = (num & 31).astype(jnp.float32) * (1.0 / 32.0)
    return (num >> 5) - base, 1.0 - far, far


def row_terms(shear_ref, depth_pos, base):
    num = shear_ref[1] * depth_pos
    far = (num & 127).astype(jnp.float32) * (1.0 / 128.0)
    return (num >> 7) - base, 1.0 - far, far


def march_rows(first, depth_idx, shear_ref, sigma, lines, turned):
    row_base = (shear_ref[1] * depth_idx) >> 3
    total = [jnp.zeros((8, LANES), jnp.float32) for _ in range(BLOCKS)]
    light = [jnp.zeros((8, LANES), jnp.float32) for _ in range(BLOCKS)]
    trans = [jnp.ones((8, LANES), jnp.float32) for _ in range(BLOCKS)]
    for i in range(SLAB):
        rel, near, far = row_terms(shear_ref, depth_idx * SLAB + i, row_base)
        near = near * -sigma
        far = far * -sigma
        start = first + HALO - rel
        for j in range(BLOCKS):
            step = near * lines[i, j, pl.ds(start, 8), :] + far * lines[i, j, pl.ds(start - 1, 8), :]
            total[j] = total[j] + step
            after = jnp.exp2(total[j])
            light[j] = light[j] + step * (trans[j] - after)
            trans[j] = after
    col_base = (shear_ref[0] * depth_idx) >> 1
    scale = -1.0 / jnp.full((8, LANES), sigma, jnp.float32)
    total = shift_columns(total, col_base)
    light = shift_columns([scale * value for value in light], col_base)
    for j in range(BLOCKS):
        turned[0, j, pl.ds(row_base + first, 8), :] = total[j]
        turned[1, j, pl.ds(row_base + first, 8), :] = light[j]


def bulk_kernel(shear_ref, ext_ref, empty_ref, first_ref, volume_ref, turned_ref, top_ref, lines):
    depth_idx = lax.axis_index("depth")
    tile_pos = lax.axis_index("tile")
    sigma = ext_ref[0] * (4.0 / 1024.0 * math.log2(math.e))
    own_count = empty_ref[0, tile_pos]
    col_base = (shear_ref[0] * depth_idx) >> 1

    @pl.loop(0, SLAB, unroll=SLAB)
    def _(i):
        rel, near, far = column_terms(shear_ref, depth_idx * SLAB + i, col_base)
        live = (i >= own_count).astype(jnp.float32)
        for c in range(ROWS // 16):
            plane = volume_ref[i, c * 16 : (c + 1) * 16, :] if c else first_ref[i]
            plane = plane.astype(jnp.float32)
            blocks = column_lerp(plane, rel, near * live, far * live)
            for j in range(BLOCKS):
                lines[i, j, HALO + c * 16 : HALO + (c + 1) * 16, :] = blocks[j]
                if c == 0:
                    top_ref[i, j] = blocks[j][:8]

    @pl.loop(1, ROWS // 8, unroll=ROWS // 8 - 1)
    def _(c):
        march_rows(c * 8, depth_idx, shear_ref, sigma, lines, turned_ref)


def edge_kernel(
    shear_ref, ext_ref, empty_ref, top_ref, above_ref, turned_ref, out_ref, lines, edge
):
    depth_idx = lax.axis_index("depth")
    tile_pos = lax.axis_index("tile")
    sigma = ext_ref[0] * (4.0 / 1024.0 * math.log2(math.e))
    above_count = empty_ref[0, jnp.maximum(tile_pos - 1, 0)]
    col_base = (shear_ref[0] * depth_idx) >> 1
    row_base = (shear_ref[1] * depth_idx) >> 3
    above = above_ref[...].astype(jnp.float32)
    for i in range(SLAB):
        rel, near, far = column_terms(shear_ref, depth_idx * SLAB + i, col_base)
        live = (i >= above_count).astype(jnp.float32)
        halos = column_lerp(above[2 * i : 2 * i + 2], rel, near * live, far * live)
        for j in range(BLOCKS):
            lines[i, j, HALO : HALO + 8, :] = top_ref[i, j]
            lines[i, j, HALO - 2 : HALO, :] = halos[j]

    march_rows(0, depth_idx, shear_ref, sigma, lines, edge)
    for g in range(ROWS // 8):
        row = lax.broadcasted_iota(jnp.int32, (8, LANES), 0) + 8 * g
        next_tile = row < row_base
        at_edge = row < row_base + 8
        rows = slice(8 * g, 8 * g + 8)
        for j in range(BLOCKS):
            total, light = [
                jnp.where(
                    next_tile,
                    turned_ref[k, j, ROWS + 8 * g : ROWS + 8 * g + 8, :],
                    jnp.where(at_edge, edge[k, j, rows, :], turned_ref[k, j, rows, :]),
                )
                for k in range(2)
            ]
            out_ref[g * BLOCKS + j] = encode_brick(total, light)


def compose_kernel(shear_ref, parts_ref, front_ref, back_ref):
    row = lax.broadcasted_iota(jnp.int32, (8, LANES), 0) + (lax.axis_index("depth") >> 3) * 8
    limit = 8 * row + 8
    slope = jnp.full((8, LANES), shear_ref[1], jnp.int32)
    zero = jnp.zeros((8, LANES), jnp.float32)
    reach = jnp.zeros((8, LANES), jnp.int32)
    total, front_total, front_light, back_light = zero, zero, zero, zero
    for d in range(DEPTH):
        codes = parts_ref[d].astype(jnp.int32)
        depth = depth_from_code(codes[:8], BRICK_RANGE)
        light = from_code(codes[8:]) * depth * jnp.exp2(-total)
        in_front = reach < limit
        front_total = jnp.where(in_front, front_total + depth, front_total)
        front_light = jnp.where(in_front, front_light + light, front_light)
        back_light = jnp.where(in_front, back_light, back_light + light)
        total = total + depth
        reach = reach + slope
    scale = math.log(2.0) / TOP
    front_ref[0:8, :] = front_total
    front_ref[8:16, :] = front_light * scale
    back_ref[0:8, :] = total - front_total
    back_ref[8:16, :] = back_light * scale * jnp.exp2(front_total)


def spread_kernel(front_ref, back_ref, out_ref):
    depth = front_ref[0:8, :] + back_ref[0:8, :]
    light = front_ref[8:16, :] + jnp.exp2(-front_ref[0:8, :]) * back_ref[8:16, :]
    opacity = 1.0 - jnp.exp2(-depth)
    mean = light / jnp.maximum(opacity, 2.0 ** IMAGE_RANGE[0])
    codes = jnp.concatenate([depth_to_code(depth, IMAGE_RANGE), to_code(mean * TOP)], axis=0)
    codes = codes.astype(jnp.int16)
    for p in range(DEPTH):
        out_ref[p] = codes


def image_kernel(palette_ref, whole_ref, image_hbm, image, sems):
    base = [palette_ref[0, k] for k in range(3)]
    slope = [palette_ref[1, k] for k in range(3)]
    copies = []
    for g in range(ROWS // 8):
        rows = slice(g * 8, (g + 1) * 8)
        for j in range(BLOCKS):
            columns = slice(j * LANES, (j + 1) * LANES)
            codes = whole_ref[g * BLOCKS + j].astype(jnp.int32)
            opacity = 1.0 - jnp.exp2(-depth_from_code(codes[:8], IMAGE_RANGE))
            light = from_code(codes[8:]) * (1.0 / TOP) * opacity
            for k in range(3):
                image[k, rows, columns] = base[k] * opacity + slope[k] * light
            image[3, rows, columns] = opacity
        part = pl.ds(g * 8, 8)
        copies.append(pltpu.make_async_copy(image.at[:, part], image_hbm.at[:, part], sems.at[g]))
        copies[-1].start()
    for copy in copies:
        copy.wait()


def call(kernel, out_shape, in_specs, scratch=(), out_specs=None):
    return pl.pallas_call(
        kernel,
        out_shape=out_shape,
        in_specs=in_specs,
        out_specs=out_specs or jax.tree.map(lambda _: VMEM, out_shape),
        scratch_shapes=list(scratch),
        compiler_params=pltpu.CompilerParams(vmem_limit_bytes=LIMIT),
    )


def per_device(volume, empty_slices, shear, extinction, palette):
    f32 = jnp.float32
    parts_shape = jax.ShapeDtypeStruct((DEPTH, 16, LANES), jnp.int16)
    piece_shape = jax.ShapeDtypeStruct((16, LANES), f32)
    down = [(i, i + 1) for i in range(TILES - 1)]
    first, last = lax.optimization_barrier((volume[:, :16, :], volume[:, ROWS - 16 :, :]))
    above = lax.ppermute(last[:, 14:, :].reshape(2 * SLAB, WIDTH), "tile", down)
    turned, top = call(
        bulk_kernel,
        (
            jax.ShapeDtypeStruct((2, BLOCKS, 2 * ROWS, LANES), f32),
            jax.ShapeDtypeStruct((SLAB, BLOCKS, 8, LANES), f32),
        ),
        [SMEM, SMEM, SMEM, VMEM, VMEM],
        [pltpu.VMEM((SLAB, BLOCKS, HALO + ROWS, LANES), f32)],
    )(shear, extinction, empty_slices, first, volume)
    parts = call(
        edge_kernel,
        parts_shape,
        [SMEM, SMEM, SMEM, VMEM, VMEM, VMEM],
        [
            pltpu.VMEM((SLAB, BLOCKS, HALO + 8, LANES), f32),
            pltpu.VMEM((2, BLOCKS, ROWS, LANES), f32),
        ],
    )(shear, extinction, empty_slices, top, above, turned)
    parts = lax.all_to_all(parts, "depth", 0, 0, tiled=True)
    front, back = call(compose_kernel, (piece_shape, piece_shape), [SMEM, VMEM])(shear, parts)
    back = lax.ppermute(back, "tile", down)
    copies = call(spread_kernel, parts_shape, [VMEM, VMEM])(front, back)
    whole = lax.all_to_all(copies, "depth", 0, 0, tiled=True)
    image_shape = jax.ShapeDtypeStruct((4, ROWS, WIDTH), f32)
    return call(
        image_kernel,
        image_shape,
        [SMEM, VMEM],
        [
            pltpu.VMEM((4, ROWS, WIDTH), f32),
            pltpu.SemaphoreType.DMA((ROWS // 8,)),
        ],
        pl.BlockSpec(memory_space=pl.ANY),
    )(palette, whole)


def solution(mesh):
    in_specs = (P("depth", "tile", None), P("depth", None), P(), P(), P())
    out_specs = P(None, "tile", None)
    return jax.shard_map(
        per_device, mesh=mesh, in_specs=in_specs, out_specs=out_specs, check_vma=False
    )
```

```python
import math

import jax
import jax.numpy as jnp
from jax import lax
from jax.experimental import pallas as pl
from jax.experimental.pallas import tpu as pltpu
from jax.sharding import PartitionSpec as P

SLAB = 16
ROWS = 64
WIDTH = 1024
LANES = 128
BLOCKS = WIDTH // LANES
DEPTH = 64
TILES = 8
HALO = 8
SMEM = pl.BlockSpec(memory_space=pltpu.SMEM)
VMEM = pl.BlockSpec(memory_space=pltpu.VMEM)
LIMIT = 48 * 1024 * 1024


TOP = 65535.0
BRICK_RANGE = (-27.0, math.log2(16 * 4 / 1024 * math.log2(math.e)) + 0.001)
IMAGE_RANGE = (-25.0, math.log2(4 * math.log2(math.e)) + 0.001)


def to_code(value):
    return (jnp.clip(value, 0.0, TOP) + 0.5).astype(jnp.int32)


def pair(above, below):
    return lax.shift_left(above, 16) | below


def unpair(codes):
    above = lax.shift_right_logical(codes, 16)
    return above.astype(jnp.float32), (codes & 0xFFFF).astype(jnp.float32)


def depth_to_code(depth, limits):
    low, high = limits
    steps = (TOP - 1.0) / (high - low)
    seen = depth >= 2.0**low
    level = (jnp.log2(jnp.where(seen, depth, 1.0)) - low) * steps + 1.0
    return to_code(jnp.where(seen, level, 0.0))


def depth_from_level(level, limits):
    low, high = limits
    depth = jnp.exp2((level - 1.0) * ((high - low) / (TOP - 1.0)) + low)
    return jnp.where(level > 0.5, depth, 0.0)


def encode_brick(total, light):
    depth = -total
    seen = depth >= 2.0 ** BRICK_RANGE[0]
    mean = light / (jnp.where(seen, depth, 1.0) * math.log(2.0))
    return pair(depth_to_code(depth, BRICK_RANGE), to_code(jnp.where(seen, mean * TOP, 0.0)))


def lane_index(rows):
    return lax.broadcasted_iota(jnp.int32, (rows, LANES), 1)


def column_lerp(plane, rel, near, far):
    rows = plane.shape[0]
    lane = lane_index(rows)
    keep_near = lane >= rel
    keep_far = lane >= rel + 1
    last_near = jnp.zeros((rows, LANES), jnp.float32)
    last_far = last_near
    out = []
    for j in range(BLOCKS):
        block = plane[:, j * LANES : (j + 1) * LANES]
        turn_near = pltpu.roll(block, rel, 1)
        turn_far = pltpu.roll(block, rel + 1, 1)
        out.append(
            near * jnp.where(keep_near, turn_near, last_near)
            + far * jnp.where(keep_far, turn_far, last_far)
        )
        last_near, last_far = turn_near, turn_far
    return out


def shift_columns(blocks, distance):
    rows = blocks[0].shape[0]
    part = distance & (LANES - 1)
    whole = jnp.full((rows, LANES), distance >> 7, jnp.int32) == 1
    own = lane_index(rows) >= part
    zero = jnp.zeros_like(blocks[0])
    turned = [pltpu.roll(block, part, 1) for block in blocks]
    placed = [jnp.where(whole, turned[j - 1] if j else zero, turned[j]) for j in range(BLOCKS)]
    return [jnp.where(own, placed[j], placed[j - 1] if j else zero) for j in range(BLOCKS)]


def column_terms(shear_ref, depth_pos, base):
    num = shear_ref[0] * depth_pos
    far = (num & 31).astype(jnp.float32) * (1.0 / 32.0)
    return (num >> 5) - base, 1.0 - far, far


def row_terms(shear_ref, depth_pos, base):
    num = shear_ref[1] * depth_pos
    far = (num & 127).astype(jnp.float32) * (1.0 / 128.0)
    return (num >> 7) - base, 1.0 - far, far


def march_rows(first, depth_idx, shear_ref, sigma, lines, turned):
    row_base = (shear_ref[1] * depth_idx) >> 3
    total = [jnp.zeros((8, LANES), jnp.float32) for _ in range(BLOCKS)]
    light = [jnp.zeros((8, LANES), jnp.float32) for _ in range(BLOCKS)]
    trans = [jnp.ones((8, LANES), jnp.float32) for _ in range(BLOCKS)]
    for i in range(SLAB):
        rel, near, far = row_terms(shear_ref, depth_idx * SLAB + i, row_base)
        near = near * -sigma
        far = far * -sigma
        start = first + HALO - rel
        for j in range(BLOCKS):
            step = near * lines[i, j, pl.ds(start, 8), :] + far * lines[i, j, pl.ds(start - 1, 8), :]
            total[j] = total[j] + step
            after = jnp.exp2(total[j])
            light[j] = light[j] + step * (trans[j] - after)
            trans[j] = after
    col_base = (shear_ref[0] * depth_idx) >> 1
    scale = -1.0 / jnp.full((8, LANES), sigma, jnp.float32)
    total = shift_columns(total, col_base)
    light = shift_columns([scale * value for value in light], col_base)
    for j in range(BLOCKS):
        turned[0, j, pl.ds(row_base + first, 8), :] = total[j]
        turned[1, j, pl.ds(row_base + first, 8), :] = light[j]


def bulk_kernel(shear_ref, ext_ref, empty_ref, first_ref, volume_ref, turned_ref, top_ref, slope_ref, lines):
    depth_idx = lax.axis_index("depth")
    tile_pos = lax.axis_index("tile")
    sigma = ext_ref[0] * (4.0 / 1024.0 * math.log2(math.e))
    own_count = empty_ref[0, tile_pos]
    col_base = (shear_ref[0] * depth_idx) >> 1

    slope_ref[...] = jnp.full((8, LANES), shear_ref[1], jnp.int32)

    @pl.loop(0, SLAB, unroll=SLAB)
    def _(i):
        rel, near, far = column_terms(shear_ref, depth_idx * SLAB + i, col_base)
        live = (i >= own_count).astype(jnp.float32)
        for c in range(ROWS // 16):
            plane = volume_ref[i, c * 16 : (c + 1) * 16, :] if c else first_ref[i]
            plane = plane.astype(jnp.float32)
            blocks = column_lerp(plane, rel, near * live, far * live)
            for j in range(BLOCKS):
                lines[i, j, HALO + c * 16 : HALO + (c + 1) * 16, :] = blocks[j]
                if c == 0:
                    top_ref[i, j] = blocks[j][:8]

    @pl.loop(1, ROWS // 8, unroll=ROWS // 8 - 1)
    def _(c):
        march_rows(c * 8, depth_idx, shear_ref, sigma, lines, turned_ref)


def edge_kernel(
    shear_ref, ext_ref, empty_ref, top_ref, above_ref, turned_ref, out_ref, lines, edge
):
    depth_idx = lax.axis_index("depth")
    tile_pos = lax.axis_index("tile")
    sigma = ext_ref[0] * (4.0 / 1024.0 * math.log2(math.e))
    above_count = empty_ref[0, jnp.maximum(tile_pos - 1, 0)]
    col_base = (shear_ref[0] * depth_idx) >> 1
    row_base = (shear_ref[1] * depth_idx) >> 3
    above = above_ref[...].astype(jnp.float32)
    for i in range(SLAB):
        rel, near, far = column_terms(shear_ref, depth_idx * SLAB + i, col_base)
        live = (i >= above_count).astype(jnp.float32)
        halos = column_lerp(above[2 * i : 2 * i + 2], rel, near * live, far * live)
        for j in range(BLOCKS):
            lines[i, j, HALO : HALO + 8, :] = top_ref[i, j]
            lines[i, j, HALO - 2 : HALO, :] = halos[j]

    march_rows(0, depth_idx, shear_ref, sigma, lines, edge)
    for g in range(ROWS // 8):
        row = lax.broadcasted_iota(jnp.int32, (8, LANES), 0) + 8 * g
        next_tile = row < row_base
        at_edge = row < row_base + 8
        rows = slice(8 * g, 8 * g + 8)
        for j in range(BLOCKS):
            total, light = [
                jnp.where(
                    next_tile,
                    turned_ref[k, j, ROWS + 8 * g : ROWS + 8 * g + 8, :],
                    jnp.where(at_edge, edge[k, j, rows, :], turned_ref[k, j, rows, :]),
                )
                for k in range(2)
            ]
            out_ref[g * BLOCKS + j] = encode_brick(total, light)


def compose_kernel(slope_ref, parts_ref, front_ref, back_ref):
    row = lax.broadcasted_iota(jnp.int32, (8, LANES), 0) + (lax.axis_index("depth") >> 3) * 8
    limit = 8 * row + 8
    slope = slope_ref[...]
    zero = jnp.zeros((8, LANES), jnp.float32)
    reach = jnp.zeros((8, LANES), jnp.int32)
    total, front_total, front_light, back_light = zero, zero, zero, zero
    for d in range(DEPTH):
        level, mean = unpair(parts_ref[d])
        depth = depth_from_level(level, BRICK_RANGE)
        light = mean * depth * jnp.exp2(-total)
        in_front = reach < limit
        front_total = jnp.where(in_front, front_total + depth, front_total)
        front_light = jnp.where(in_front, front_light + light, front_light)
        back_light = jnp.where(in_front, back_light, back_light + light)
        total = total + depth
        reach = reach + slope
    scale = math.log(2.0) / TOP
    front_ref[0:8, :] = front_total
    front_ref[8:16, :] = front_light * scale
    back_ref[0:8, :] = total - front_total
    back_ref[8:16, :] = back_light * scale * jnp.exp2(front_total)


def spread_kernel(front_ref, back_ref, out_ref):
    depth = front_ref[0:8, :] + back_ref[0:8, :]
    light = front_ref[8:16, :] + jnp.exp2(-front_ref[0:8, :]) * back_ref[8:16, :]
    opacity = 1.0 - jnp.exp2(-depth)
    mean = light / jnp.maximum(opacity, 2.0 ** IMAGE_RANGE[0])
    codes = pair(depth_to_code(depth, IMAGE_RANGE), to_code(mean * TOP))
    for p in range(DEPTH):
        out_ref[p] = codes


def image_kernel(palette_ref, whole_ref, image_hbm, image, sems):
    base, slope = [
        [jnp.broadcast_to(palette_ref[i : i + 1, k : k + 1], (8, LANES)) for k in range(3)]
        for i in range(2)
    ]
    copies = []
    for g in range(ROWS // 8):
        rows = slice(g * 8, (g + 1) * 8)
        for j in range(BLOCKS):
            columns = slice(j * LANES, (j + 1) * LANES)
            level, mean = unpair(whole_ref[g * BLOCKS + j])
            opacity = 1.0 - jnp.exp2(-depth_from_level(level, IMAGE_RANGE))
            light = mean * (1.0 / TOP) * opacity
            for k in range(3):
                image[k, rows, columns] = base[k] * opacity + slope[k] * light
            image[3, rows, columns] = opacity
        part = pl.ds(g * 8, 8)
        copies.append(pltpu.make_async_copy(image.at[:, part], image_hbm.at[:, part], sems.at[g]))
        copies[-1].start()
    for copy in copies:
        copy.wait()


def call(kernel, out_shape, in_specs, scratch=(), out_specs=None):
    return pl.pallas_call(
        kernel,
        out_shape=out_shape,
        in_specs=in_specs,
        out_specs=out_specs or jax.tree.map(lambda _: VMEM, out_shape),
        scratch_shapes=list(scratch),
        compiler_params=pltpu.CompilerParams(vmem_limit_bytes=LIMIT),
    )


def per_device(volume, empty_slices, shear, extinction, palette):
    f32 = jnp.float32
    parts_shape = jax.ShapeDtypeStruct((DEPTH, 8, LANES), jnp.int32)
    piece_shape = jax.ShapeDtypeStruct((16, LANES), f32)
    down = [(i, i + 1) for i in range(TILES - 1)]
    first, last = lax.optimization_barrier((volume[:, :16, :], volume[:, ROWS - 16 :, :]))
    above = lax.ppermute(last[:, 14:, :].reshape(2 * SLAB, WIDTH), "tile", down)
    turned, top, slope = call(
        bulk_kernel,
        (
            jax.ShapeDtypeStruct((2, BLOCKS, 2 * ROWS, LANES), f32),
            jax.ShapeDtypeStruct((SLAB, BLOCKS, 8, LANES), f32),
            jax.ShapeDtypeStruct((8, LANES), jnp.int32),
        ),
        [SMEM, SMEM, SMEM, VMEM, VMEM],
        [pltpu.VMEM((SLAB, BLOCKS, HALO + ROWS, LANES), f32)],
    )(shear, extinction, empty_slices, first, volume)
    parts = call(
        edge_kernel,
        parts_shape,
        [SMEM, SMEM, SMEM, VMEM, VMEM, VMEM],
        [
            pltpu.VMEM((SLAB, BLOCKS, HALO + 8, LANES), f32),
            pltpu.VMEM((2, BLOCKS, ROWS, LANES), f32),
        ],
    )(shear, extinction, empty_slices, top, above, turned)
    parts = lax.all_to_all(parts, "depth", 0, 0, tiled=True)
    front, back = call(compose_kernel, (piece_shape, piece_shape), [VMEM, VMEM])(slope, parts)
    back = lax.ppermute(back, "tile", down)
    copies = call(spread_kernel, parts_shape, [VMEM, VMEM])(front, back)
    whole = lax.all_to_all(copies, "depth", 0, 0, tiled=True)
    image_shape = jax.ShapeDtypeStruct((4, ROWS, WIDTH), f32)
    return call(
        image_kernel,
        image_shape,
        [VMEM, VMEM],
        [
            pltpu.VMEM((4, ROWS, WIDTH), f32),
            pltpu.SemaphoreType.DMA((ROWS // 8,)),
        ],
        pl.BlockSpec(memory_space=pl.ANY),
    )(palette, whole)


def solution(mesh):
    in_specs = (P("depth", "tile", None), P("depth", None), P(), P(), P())
    out_specs = P(None, "tile", None)
    return jax.shard_map(
        per_device, mesh=mesh, in_specs=in_specs, out_specs=out_specs, check_vma=False
    )
```
